32 devices in a mesh: groups: 2 (over y), blk: 8 (over z, x), proj: 2 (over core).
Axes of the slice: x: 2, y: 2, z: 4, core: 2. Of those that a mesh axis runs over, the one named last changes fastest.
Arguments:
- documents: bfloat16 [6144, 8192], P(('groups', 'blk'), 'proj'), parts along dimension 0, may hold values from -60 to 60
- queries: bfloat16 [192, 8192], P(('groups', 'blk'), 'proj'), parts along dimension 0, may hold values from -60 to 60
- preconditioner: float32 [8192], P('proj'), may hold values from 0.1 to 3
Outputs:
- scores: float32 [6144, 96], P(('groups', 'blk', 'proj')), parts along dimension 0
The draws below stay inside these ranges and needn't reach their ends.
There are 2 independent parts, one for each index of `groups`. The reference program is written for one: setup_inputs(seed, part) draws one part's arguments, and reference() takes and returns one part's arrays. A program takes and returns all parts, laid end to end along the dimension named above; an argument that names none is the same for every part. Nothing has to cross between parts.
All inputs are finite; a program needn't handle non-finite values.
Results may differ from the reference program's by a relative error of at most 0.009.
Values may be sent and summed in bfloat16 or wider, within the bound.
No kernel may reach another device: no remote copies, remote signals or barrier semaphores. Data moves between devices by JAX's collectives and lax.ppermute only.
A program may use at most 128 MiB of HBM per device.

```python
import math
import jax
import jax.numpy as jnp
from jax import lax

PROJ = 8192
DOC_DEV = 384
DOCS = 3072
QUERIES = 96
N_BLK = 8


def gradient_rows(key, count):
    key_scale, key_entries = jax.random.split(key)
    row_scales = jnp.exp(jax.random.uniform(key_scale, (count, 1), jnp.float32) * jnp.log(10.0))
    entries = jnp.clip(jax.random.normal(key_entries, (count, PROJ), jnp.float32), -6.0, 6.0)
    return (row_scales * entries).astype(jnp.bfloat16)


def draw_documents(key, part):
    key = jax.random.fold_in(key, 1)
    return gradient_rows(key, DOCS)


def draw_queries(key, part):
    key = jax.random.fold_in(key, 2)
    return gradient_rows(key, QUERIES)


def level_of(stream_key, dims, cuts, least, top_value):
    level = 1.0
    for position, shards_of in cuts:
        draws = jax.random.uniform(jax.random.fold_in(jax.random.fold_in(stream_key, 6), position), (shards_of,), jnp.float32, least / len(cuts), top_value / len(cuts))
        level = level * jnp.repeat(jnp.exp(draws), dims[position] // shards_of).reshape((-1,) + (1,) * (len(dims) - 1 - position))
    return level


def setup_inputs(seed: int = 0, part: int = 0) -> dict:
    key_of = jax.random.split(jax.random.key(seed), 4)
    own_keys = jax.random.split(jax.random.fold_in(key_of[3], part), 4)
    return {
        "documents": draw_documents(jax.random.fold_in(jax.random.fold_in(key_of[3], part), 71), part),
        "queries": draw_queries(jax.random.fold_in(jax.random.fold_in(key_of[3], part), 71), part),
        "preconditioner": jnp.clip(jnp.exp(math.log(3.0) - 3.4011974 * jax.random.uniform(key_of[2], (PROJ,), jnp.float32) ** level_of(key_of[2], (PROJ,), ((0, 2),), -0.2, 0.2)), 0.1, 3.0),
    }


def reference(documents, queries, preconditioner):
    weighted = (queries.astype(jnp.float32) * preconditioner[None, :]).astype(jnp.bfloat16)
    wide_weighted = weighted.astype(jnp.float32)
    query_squares = jnp.einsum('qp,qp->q', wide_weighted, wide_weighted)
    query_scale = lax.rsqrt(query_squares / PROJ + 1e-06)
    grouped = documents.reshape(N_BLK, DOC_DEV, PROJ)

    def score_group(doc_block):
        wide_block = doc_block.astype(jnp.float32)
        squares = jnp.einsum('dp,dp->d', wide_block, wide_block)
        doc_scale = lax.rsqrt(squares / PROJ + 1e-06)
        raw_scores = jnp.dot(doc_block, weighted.T, preferred_element_type=jnp.float32)
        return raw_scores * doc_scale[:, None] * query_scale[None, :] / math.sqrt(PROJ)
    return lax.map(score_group, grouped).reshape(DOCS, QUERIES)
```

```python
import functools
import math

import jax
import jax.numpy as jnp
from jax import lax
from jax.experimental import pallas as pl
from jax.experimental.pallas import tpu as pltpu
from jax.sharding import PartitionSpec as P

EPS = 1e-06
VMEM_LIMIT = 24 * 1024 * 1024
BOTH = ("blk", "proj")
NT = (((1,), (1,)), ((), ()))


def params():
    return pltpu.CompilerParams(vmem_limit_bytes=VMEM_LIMIT)


def vmem():
    return pl.BlockSpec(memory_space=pltpu.VMEM)


def smem():
    return pl.BlockSpec(memory_space=pltpu.SMEM)


def pack_kernel(queries, preconditioner, packed):
    width = packed.shape[1]
    third = width // 3
    weighted = queries[...].astype(jnp.float32) * preconditioner[...]
    tail = jnp.concatenate([weighted[4 * k : 4 * k + 4, width:] for k in range(3)], axis=1)
    packed[...] = jnp.concatenate([weighted[:, :width], tail], axis=0).astype(packed.dtype)


def unpack(packed):
    width = packed.shape[1]
    third = width // 3
    wide = packed.astype(jnp.float32)
    tail = jnp.concatenate(
        [wide[12:16, k * third : (k + 1) * third] for k in range(3)]
        + [jnp.zeros((4, third), jnp.float32)],
        axis=0,
    )
    row = lax.broadcasted_iota(jnp.int32, wide.shape, 0)
    head = jnp.where(row < 12, wide, 0.0)
    return jnp.concatenate([head, tail], axis=1).astype(jnp.bfloat16)


def squares_kernel(documents, squares):
    wide = documents[...].astype(jnp.float32)
    squares[...] = jnp.sum(wide * wide, axis=1, keepdims=True)


def early_kernel(place, documents, squares, *rest):
    pieces, (scores, query_squares, whole) = rest[:-3], rest[-3:]
    whole[...] = jnp.zeros_like(whole)
    for s, piece in enumerate(pieces):
        whole[pl.ds(pl.multiple_of(place[s] * 16, 16), 16), :] = unpack(piece[...])
    lane = lax.broadcasted_iota(jnp.int32, scores.shape, 1)
    raw = lax.dot_general(documents[...], whole[...], NT, preferred_element_type=jnp.float32)
    scores[...] = jnp.where(lane == 12, squares[...], raw)
    own = lax.dot_general(whole[...], whole[...], NT, preferred_element_type=jnp.float32)
    eye = lax.broadcasted_iota(jnp.int32, own.shape, 0) == lax.broadcasted_iota(jnp.int32, own.shape, 1)
    query_squares[...] = jnp.broadcast_to(
        jnp.sum(jnp.where(eye, own, 0.0), axis=0, keepdims=True), query_squares.shape
    )


def spread(narrow, place, width):
    wide = jnp.concatenate(
        [narrow, jnp.zeros((narrow.shape[0], width - narrow.shape[1]), jnp.float32)], axis=1
    )
    return pltpu.roll(wide, place * 16, 1)


def late_kernel(place, documents, piece, scores, query_squares, keep, send):
    half = keep.shape[0] - 8
    width = keep.shape[1]
    last = unpack(piece[...])
    own = lax.dot_general(last, last, NT, preferred_element_type=jnp.float32)
    eye = lax.broadcasted_iota(jnp.int32, own.shape, 0) == lax.broadcasted_iota(jnp.int32, own.shape, 1)
    own = jnp.broadcast_to(jnp.sum(jnp.where(eye, own, 0.0), axis=0, keepdims=True), (8, 16))
    row = query_squares[...] + spread(own, place[0], width)
    for to, core in ((send, 1 - place[1]), (keep, place[1])):
        rows = pl.ds(pl.multiple_of(core * half, 16), half)
        raw = lax.dot_general(documents[rows, :], last, NT, preferred_element_type=jnp.float32)
        to[:half, :] = scores[rows, :] + spread(raw, place[0], width)
        to[half:, :] = row


def finish_kernel(coordinates, keep, got, scores):
    half = scores.shape[0]
    total = keep[...] + got[...]
    doc_scale = lax.rsqrt(total[:half, 12:13] / coordinates + EPS)
    query_scale = lax.rsqrt(total[half : half + 1, :] / coordinates + EPS) / math.sqrt(coordinates)
    scaled = total[:half] * doc_scale * query_scale
    scores[...] = jnp.concatenate(
        [scaled[:, 16 * j : 16 * j + 12] for j in range(scores.shape[1] // 12)], axis=1
    )


def squared_paths(blocks):
    one = [(b, b ^ 1) for b in range(blocks)]
    two = [(b, b ^ 2) for b in range(blocks)]
    far = [(b, b ^ 4) for b in range(blocks)]
    first = [(2 * b, 2 * c) for b, c in two] + [(2 * b + 1, 2 * c + 1) for b, c in one]
    second = [(2 * b, 2 * c) for b, c in one] + [(2 * b + 1, 2 * c + 1) for b, c in two]
    return far, first, second


def by_squares(documents, queries, preconditioner):
    docs, width = documents.shape
    blocks = lax.axis_size("blk")
    half = docs // 2
    me, core = lax.axis_index("blk"), lax.axis_index("proj")
    far, first, second = squared_paths(blocks)
    packed = pl.pallas_call(
        pack_kernel,
        out_shape=jax.ShapeDtypeStruct((16, 3 * width // 4), jnp.bfloat16),
        in_specs=[vmem()] * 2,
        out_specs=vmem(),
        compiler_params=params(),
        name="pack",
    )(queries, preconditioner.reshape(1, width))
    squares = pl.pallas_call(
        squares_kernel,
        out_shape=jax.ShapeDtypeStruct((docs, 1), jnp.float32),
        in_specs=[vmem()],
        out_specs=vmem(),
        compiler_params=params(),
        name="squares",
    )(documents)
    across = lax.ppermute(packed, "blk", far)
    n1 = lax.ppermute(packed, BOTH, first)
    n2 = lax.ppermute(packed, BOTH, second)
    n3 = lax.ppermute(n1, BOTH, second)
    a1 = lax.ppermute(across, BOTH, first)
    a2 = lax.ppermute(across, BOTH, second)
    a3 = lax.ppermute(a1, BOTH, second)
    early = [packed, n1, n2, n3, across, a1, a2]
    m1, m2 = 2 - core, 1 + core
    zero = jnp.zeros_like(me)
    places = jnp.stack([me, me ^ m1, me ^ m2, me ^ 3, me ^ 4, me ^ 4 ^ m1, me ^ 4 ^ m2]).astype(jnp.int32)
    scores, query_squares = pl.pallas_call(
        early_kernel,
        out_shape=(
            jax.ShapeDtypeStruct((docs, 16 * blocks), jnp.float32),
            jax.ShapeDtypeStruct((8, 16 * blocks), jnp.float32),
        ),
        in_specs=[smem()] + [vmem()] * (2 + len(early)),
        out_specs=(vmem(), vmem()),
        scratch_shapes=[pltpu.VMEM((16 * blocks, width), jnp.bfloat16)],
        compiler_params=params(),
        name="early",
    )(places, documents, squares, *early)
    message = jax.ShapeDtypeStruct((half + 8, 16 * blocks), jnp.float32)
    keep, send = pl.pallas_call(
        late_kernel,
        out_shape=(message, message),
        in_specs=[smem()] + [vmem()] * 4,
        out_specs=(vmem(), vmem()),
        compiler_params=params(),
        name="late",
    )(jnp.stack([me ^ 7, core]).astype(jnp.int32), documents, a3, scores, query_squares)
    got = lax.ppermute(send, "proj", [(0, 1), (1, 0)])
    return pl.pallas_call(
        functools.partial(finish_kernel, 2 * width),
        out_shape=jax.ShapeDtypeStruct((half, 12 * blocks), jnp.float32),
        in_specs=[vmem()] * 2,
        out_specs=vmem(),
        compiler_params=params(),
        name="finish",
    )(keep, got)


def by_gather(documents, queries, preconditioner):
    docs, width = documents.shape
    coordinates = width * lax.axis_size("proj")
    half = docs // lax.axis_size("proj")
    weighted = (queries.astype(jnp.float32) * preconditioner[None, :]).astype(jnp.bfloat16)
    everyone = lax.all_gather(weighted, "blk", axis=0, tiled=True)
    raw = lax.dot_general(documents, everyone, NT, preferred_element_type=jnp.float32)
    doc_squares = jnp.einsum("dp,dp->d", documents, documents, preferred_element_type=jnp.float32)
    query_squares = jnp.einsum("qp,qp->q", everyone, everyone, preferred_element_type=jnp.float32)
    doc_squares, query_squares = lax.psum((doc_squares, query_squares), "proj")
    raw = lax.psum_scatter(raw, "proj", scatter_dimension=0, tiled=True)
    mine = lax.dynamic_slice_in_dim(doc_squares, lax.axis_index("proj") * half, half, 0)
    doc_scale = lax.rsqrt(mine / coordinates + EPS)
    query_scale = lax.rsqrt(query_squares / coordinates + EPS)
    return raw * doc_scale[:, None] * query_scale[None, :] / math.sqrt(coordinates)


def on_device(documents, queries, preconditioner):
    rows, width = queries.shape
    squares = lax.axis_size("blk") == 8 and lax.axis_size("proj") == 2
    if squares and rows == 12 and width % 512 == 0 and documents.shape[0] % 32 == 0:
        return by_squares(documents, queries, preconditioner)
    return by_gather(documents, queries, preconditioner)


def solution(mesh):
    placed = (P(("groups", "blk"), "proj"), P(("groups", "blk"), "proj"), P("proj"))
    return jax.shard_map(
        on_device,
        mesh=mesh,
        in_specs=placed,
        out_specs=P(("groups", "blk", "proj"), None),
        check_vma=False,
    )
```

```python
import functools
import math

import jax
import jax.numpy as jnp
from jax import lax
from jax.experimental import pallas as pl
from jax.experimental.pallas import tpu as pltpu
from jax.sharding import PartitionSpec as P

EPS = 1e-06
MIB = 1024 * 1024
BOTH = ("blk", "proj")
NT = (((1,), (1,)), ((), ()))


def vmem():
    return pl.BlockSpec(memory_space=pltpu.VMEM)


def smem():
    return pl.BlockSpec(memory_space=pltpu.SMEM)


def anywhere():
    return pl.BlockSpec(memory_space=pl.ANY)


def pack_kernel(queries_hbm, preconditioner_hbm, packed, queries, preconditioner, arrived):
    copies = [
        pltpu.make_async_copy(queries_hbm, queries, arrived.at[0]),
        pltpu.make_async_copy(preconditioner_hbm, preconditioner, arrived.at[1]),
    ]
    for copy in copies:
        copy.start()
    for copy in copies:
        copy.wait()
    width = queries.shape[1]
    weighted = queries[...].astype(jnp.float32) * preconditioner[...]
    packed[:, :width] = weighted[:8].astype(packed.dtype)
    tail = jnp.concatenate([weighted[8:, : width // 2], weighted[8:, width // 2 :]], axis=0)
    packed[:, width:] = tail.astype(packed.dtype)


def join_kernel(first, second, joined):
    rows = first.shape[0]
    joined[:rows] = first[...]
    joined[rows:] = second[...]


def squares_kernel(documents, squares):
    wide = documents[...].astype(jnp.float32)
    squares[...] = jnp.sum(wide * wide, axis=1, keepdims=True)


def blocks_from(steps):
    me, core = lax.axis_index("blk"), lax.axis_index("proj")
    return [me ^ (step if isinstance(step, int) else step[0] + (step[1] - step[0]) * core) for step in steps]


def unpack(packed):
    width = 2 * packed.shape[1] // 3
    tail = packed[:, width:]
    return jnp.concatenate([packed[:, :width], jnp.concatenate([tail, tail], axis=1)], axis=0)


def scatter(places, pieces, whole):
    whole[...] = jnp.zeros_like(whole)
    for place, piece in zip(places, pieces):
        whole[pl.ds(pl.multiple_of(place * 16, 16), 16), :] = unpack(piece)


def products(left, whole):
    middle = whole.shape[1] // 2
    low = lax.dot_general(left[:, :middle], whole[:, :middle], NT, preferred_element_type=jnp.float32)
    high = lax.dot_general(left[:, middle:], whole[:, middle:], NT, preferred_element_type=jnp.float32)
    lane = lax.broadcasted_iota(jnp.int32, low.shape, 1) & 15
    moved = pltpu.roll(high, low.shape[1] - 4, 1)
    return jnp.where(lane < 8, low + high, jnp.where(lane < 12, low + moved, 0.0))


def own_squares(places, pieces, lanes):
    lane = lax.broadcasted_iota(jnp.int32, (8, lanes), 1)
    row = lax.broadcasted_iota(jnp.int32, (8, lanes), 0)
    total = jnp.zeros((8, lanes), jnp.float32)
    for place, piece in zip(places, pieces):
        width = 2 * piece.shape[1] // 3
        wide = piece.astype(jnp.float32)
        wide = wide * wide
        head = jnp.sum(wide[:, :width], axis=1, keepdims=True)
        tail = jnp.sum(wide[:, width:], axis=1, keepdims=True)
        total += jnp.where(lane == place * 16 + row, head, 0.0)
        total += jnp.where(lane == place * 16 + 8 + (row & 3), tail, 0.0)
    return jnp.broadcast_to(jnp.sum(total, axis=0, keepdims=True), (8, lanes))


def early_kernel(steps, documents, squares, *rest):
    refs, (scores, query_squares, whole) = rest[:-3], rest[-3:]
    places, pieces = blocks_from(steps), [ref[r : r + 8] for ref in refs for r in range(0, ref.shape[0], 8)]
    scatter(places, pieces, whole)
    lane = lax.broadcasted_iota(jnp.int32, scores.shape, 1)
    scores[...] = jnp.where(lane == 12, squares[...], products(documents, whole))
    query_squares[...] = own_squares(places, pieces, scores.shape[1])


def late_kernel(steps, other, documents, *rest):
    refs, (scores, query_squares, out, whole) = rest[:-4], rest[-4:]
    half = out.shape[0] - 8
    places, pieces = blocks_from(steps), [ref[r : r + 8] for ref in refs for r in range(0, ref.shape[0], 8)]
    scatter(places, pieces, whole)
    core = lax.axis_index("proj")
    side = 1 - core if other else core
    rows = pl.ds(pl.multiple_of(side * half, 16), half)
    out[:half, :] = scores[rows, :] + products(documents.at[rows], whole)
    out[half:, :] = query_squares[...] + own_squares(places, pieces, out.shape[1])


def finish_kernel(coordinates, keep, got, scores):
    half = scores.shape[0]
    total = keep[...] + got[...]
    doc_scale = lax.rsqrt(total[:half, 12:13] / coordinates + EPS)
    query_scale = lax.rsqrt(total[half : half + 1, :] / coordinates + EPS) / math.sqrt(coordinates)
    scaled = total[:half] * doc_scale * query_scale
    scores[...] = jnp.concatenate(
        [scaled[:, 16 * j : 16 * j + 12] for j in range(scores.shape[1] // 12)], axis=1
    )


def squared_paths(blocks):
    one = [(b, b ^ 1) for b in range(blocks)]
    two = [(b, b ^ 2) for b in range(blocks)]
    far = [(b, b ^ 4) for b in range(blocks)]
    first = [(2 * b, 2 * c) for b, c in two] + [(2 * b + 1, 2 * c + 1) for b, c in one]
    second = [(2 * b, 2 * c) for b, c in one] + [(2 * b + 1, 2 * c + 1) for b, c in two]
    farthest = [(b, b ^ 7) for b in range(blocks)]
    return far, farthest, first, second


def call(kernel, name, out, *args, hbm=False, scratch=(), limit=24):
    return pl.pallas_call(
        kernel,
        out_shape=out,
        in_specs=[anywhere() if hbm else vmem()] * len(args),
        out_specs=jax.tree.map(lambda _: vmem(), out),
        scratch_shapes=scratch,
        compiler_params=pltpu.CompilerParams(vmem_limit_bytes=limit * MIB),
        name=name,
        cost_estimate=pl.CostEstimate(flops=int({"early":2e10,"squares":2e10}.get(name, 1e9)), bytes_accessed=4194304, transcendentals=0),
    )(*args)


def by_squares(documents, queries, preconditioner):
    docs, width = documents.shape
    blocks = lax.axis_size("blk")
    half = docs // 2
    lanes = 16 * blocks
    far, farthest, first, second = squared_paths(blocks)
    packed = call(
        pack_kernel,
        "pack",
        pltpu.VMEM((8, 3 * width // 2), jnp.bfloat16),
        queries,
        preconditioner.reshape(1, width),
        hbm=True,
        limit=24,
        scratch=[
            pltpu.VMEM(queries.shape, queries.dtype),
            pltpu.VMEM((1, width), jnp.float32),
            pltpu.SemaphoreType.DMA((2,)),
        ],
    )
    across = lax.ppermute(packed, "blk", far)
    n1 = lax.ppermute(packed, BOTH, first)
    n2 = lax.ppermute(packed, BOTH, second)
    corner = lax.ppermute(packed, "blk", farthest)
    squares = call(squares_kernel, "squares", pltpu.VMEM((docs, 1), jnp.float32), documents)
    across, n1, n2, squares = lax.optimization_barrier((across, n1, n2, squares))
    a1 = lax.ppermute(across, BOTH, first)
    two = call(join_kernel, "join", pltpu.VMEM((16, 3 * width // 2), jnp.bfloat16), n1, across)
    pair = lax.ppermute(two, BOTH, second)
    whole = pltpu.VMEM((lanes, width), jnp.bfloat16)
    scores, query_squares = call(
        functools.partial(early_kernel, (0, (1, 2), (2, 1), 4)),
        "early",
        (pltpu.VMEM((docs, lanes), jnp.float32), pltpu.VMEM((8, lanes), jnp.float32)),
        documents,
        squares,
        packed,
        n2,
        two,
        scratch=[whole],
    )
    send, keep = (
        call(
            functools.partial(late_kernel, (7, (6, 5), 3, (5, 6)), other),
            "late",
            pltpu.VMEM((half + 8, lanes), jnp.float32),
            documents,
            corner,
            a1,
            pair,
            scores,
            query_squares,
            scratch=[whole],
        )
        for other in (True, False)
    )
    got = lax.ppermute(send, "proj", [(0, 1), (1, 0)])
    return call(
        functools.partial(finish_kernel, 2 * width),
        "finish",
        jax.ShapeDtypeStruct((half, 12 * blocks), jnp.float32),
        keep,
        got,
    )


def by_gather(documents, queries, preconditioner):
    docs, width = documents.shape
    coordinates = width * lax.axis_size("proj")
    half = docs // lax.axis_size("proj")
    weighted = (queries.astype(jnp.float32) * preconditioner[None, :]).astype(jnp.bfloat16)
    everyone = lax.all_gather(weighted, "blk", axis=0, tiled=True)
    raw = lax.dot_general(documents, everyone, NT, preferred_element_type=jnp.float32)
    doc_squares = jnp.einsum("dp,dp->d", documents, documents, preferred_element_type=jnp.float32)
    query_squares = jnp.einsum("qp,qp->q", everyone, everyone, preferred_element_type=jnp.float32)
    doc_squares, query_squares = lax.psum((doc_squares, query_squares), "proj")
    raw = lax.psum_scatter(raw, "proj", scatter_dimension=0, tiled=True)
    mine = lax.dynamic_slice_in_dim(doc_squares, lax.axis_index("proj") * half, half, 0)
    doc_scale = lax.rsqrt(mine / coordinates + EPS)
    query_scale = lax.rsqrt(query_squares / coordinates + EPS)
    return raw * doc_scale[:, None] * query_scale[None, :] / math.sqrt(coordinates)


def on_device(documents, queries, preconditioner):
    rows, width = queries.shape
    squares = lax.axis_size("blk") == 8 and lax.axis_size("proj") == 2
    if squares and rows == 12 and width % 512 == 0 and documents.shape[0] % 32 == 0:
        return by_squares(documents, queries, preconditioner)
    return by_gather(documents, queries, preconditioner)


def solution(mesh):
    placed = (P(("groups", "blk"), "proj"), P(("groups", "blk"), "proj"), P("proj"))
    return jax.shard_map(
        on_device,
        mesh=mesh,
        in_specs=placed,
        out_specs=P(("groups", "blk", "proj"), None),
        check_vma=False,
    )
```

```python
import functools
import math

import jax
import jax.numpy as jnp
from jax import lax
from jax.experimental import pallas as pl
from jax.experimental.pallas import tpu as pltpu
from jax.sharding import PartitionSpec as P

EPS = 1e-06
MIB = 1024 * 1024
BOTH = ("blk", "proj")
NT = (((1,), (1,)), ((), ()))


def vmem():
    return pl.BlockSpec(memory_space=pltpu.VMEM)


def smem():
    return pl.BlockSpec(memory_space=pltpu.SMEM)


def anywhere():
    return pl.BlockSpec(memory_space=pl.ANY)


def pack_kernel(queries_hbm, preconditioner_hbm, packed, queries, preconditioner, arrived):
    copies = [
        pltpu.make_async_copy(queries_hbm, queries, arrived.at[0]),
        pltpu.make_async_copy(preconditioner_hbm, preconditioner, arrived.at[1]),
    ]
    for copy in copies:
        copy.start()
    for copy in copies:
        copy.wait()
    width = queries.shape[1]
    weighted = queries[...].astype(jnp.float32) * preconditioner[...]
    packed[:, :width] = weighted[:8].astype(packed.dtype)
    tail = jnp.concatenate([weighted[8:, : width // 2], weighted[8:, width // 2 :]], axis=0)
    packed[:, width:] = tail.astype(packed.dtype)


def join_kernel(first, second, joined):
    rows = first.shape[0]
    joined[:rows] = first[...]
    joined[rows:] = second[...]


def squares_kernel(documents, squares):
    wide = documents[...].astype(jnp.float32)
    squares[...] = jnp.sum(wide * wide, axis=1, keepdims=True)


def blocks_from(steps):
    me, core = lax.axis_index("blk"), lax.axis_index("proj")
    return [me ^ (step if isinstance(step, int) else step[0] + (step[1] - step[0]) * core) for step in steps]


def unpack(packed):
    width = 2 * packed.shape[1] // 3
    tail = packed[:, width:]
    return jnp.concatenate([packed[:, :width], jnp.concatenate([tail, tail], axis=1)], axis=0)


def scatter(places, pieces, whole):
    whole[...] = jnp.zeros_like(whole)
    for place, piece in zip(places, pieces):
        whole[pl.ds(pl.multiple_of(place * 16, 16), 16), :] = unpack(piece)


def products(left, whole):
    middle = whole.shape[1] // 2
    low = lax.dot_general(left[:, :middle], whole[:, :middle], NT, preferred_element_type=jnp.float32)
    high = lax.dot_general(left[:, middle:], whole[:, middle:], NT, preferred_element_type=jnp.float32)
    lane = lax.broadcasted_iota(jnp.int32, low.shape, 1) & 15
    moved = pltpu.roll(high, low.shape[1] - 4, 1)
    return jnp.where(lane < 8, low + high, jnp.where(lane < 12, low + moved, 0.0))


def own_squares(places, pieces, lanes):
    lane = lax.broadcasted_iota(jnp.int32, (8, lanes), 1)
    row = lax.broadcasted_iota(jnp.int32, (8, lanes), 0)
    total = jnp.zeros((8, lanes), jnp.float32)
    for place, piece in zip(places, pieces):
        width = 2 * piece.shape[1] // 3
        wide = piece.astype(jnp.float32)
        wide = wide * wide
        head = jnp.sum(wide[:, :width], axis=1, keepdims=True)
        tail = jnp.sum(wide[:, width:], axis=1, keepdims=True)
        total += jnp.where(lane == place * 16 + row, head, 0.0)
        total += jnp.where(lane == place * 16 + 8 + (row & 3), tail, 0.0)
    return jnp.broadcast_to(jnp.sum(total, axis=0, keepdims=True), (8, lanes))


def early_kernel(steps, documents, squares, *rest):
    refs, (scores, query_squares, whole) = rest[:-3], rest[-3:]
    places, pieces = blocks_from(steps), [ref[r : r + 8] for ref in refs for r in range(0, ref.shape[0], 8)]
    scatter(places, pieces, whole)
    lane = lax.broadcasted_iota(jnp.int32, scores.shape, 1)
    scores[...] = jnp.where(lane == 12, squares[...], products(documents, whole))
    query_squares[...] = own_squares(places, pieces, scores.shape[1])


def late_kernel(steps, other, documents, *rest):
    refs, (scores, query_squares, out, whole) = rest[:-4], rest[-4:]
    half = out.shape[0] - 8
    places, pieces = blocks_from(steps), [ref[r : r + 8] for ref in refs for r in range(0, ref.shape[0], 8)]
    scatter(places, pieces, whole)
    core = lax.axis_index("proj")
    side = 1 - core if other else core
    rows = pl.ds(pl.multiple_of(side * half, 16), half)
    out[:half, :] = scores[rows, :] + products(documents.at[rows], whole)
    out[half:, :] = query_squares[...] + own_squares(places, pieces, out.shape[1])


def finish_kernel(coordinates, keep, got, scores):
    half = scores.shape[0]
    total = keep[...] + got[...]
    doc_scale = lax.rsqrt(total[:half, 12:13] / coordinates + EPS)
    query_scale = lax.rsqrt(total[half : half + 1, :] / coordinates + EPS) / math.sqrt(coordinates)
    scaled = total[:half] * doc_scale * query_scale
    scores[...] = jnp.concatenate(
        [scaled[:, 16 * j : 16 * j + 12] for j in range(scores.shape[1] // 12)], axis=1
    )


def squared_paths(blocks):
    one = [(b, b ^ 1) for b in range(blocks)]
    two = [(b, b ^ 2) for b in range(blocks)]
    far = [(b, b ^ 4) for b in range(blocks)]
    first = [(2 * b, 2 * c) for b, c in two] + [(2 * b + 1, 2 * c + 1) for b, c in one]
    second = [(2 * b, 2 * c) for b, c in one] + [(2 * b + 1, 2 * c + 1) for b, c in two]
    farthest = [(b, b ^ 7) for b in range(blocks)]
    return far, farthest, first, second


def call(kernel, name, out, *args, hbm=False, scratch=(), limit=24):
    return pl.pallas_call(
        kernel,
        out_shape=out,
        in_specs=[anywhere() if hbm else vmem()] * len(args),
        out_specs=jax.tree.map(lambda _: vmem(), out),
        scratch_shapes=scratch,
        compiler_params=pltpu.CompilerParams(vmem_limit_bytes=limit * MIB),
        name=name,
        cost_estimate=pl.CostEstimate(flops=int({"early":2e10,"squares":2e10}.get(name, 1e9)), bytes_accessed=4194304, transcendentals=0),
    )(*args)


def by_squares(documents, queries, preconditioner):
    docs, width = documents.shape
    blocks = lax.axis_size("blk")
    half = docs // 2
    lanes = 16 * blocks
    far, farthest, first, second = squared_paths(blocks)
    packed = call(
        pack_kernel,
        "pack",
        pltpu.VMEM((8, 3 * width // 2), jnp.bfloat16),
        queries,
        preconditioner.reshape(1, width),
        hbm=True,
        limit=56,
        scratch=[
            pltpu.VMEM(queries.shape, queries.dtype),
            pltpu.VMEM((1, width), jnp.float32),
            pltpu.SemaphoreType.DMA((2,)),
        ],
    )
    across = lax.ppermute(packed, "blk", far)
    n1 = lax.ppermute(packed, BOTH, first)
    n2 = lax.ppermute(packed, BOTH, second)
    corner = lax.ppermute(packed, "blk", farthest)
    squares = call(squares_kernel, "squares", pltpu.VMEM((docs, 1), jnp.float32), documents)
    across, squares = lax.optimization_barrier((across, squares))
    a1 = lax.ppermute(across, BOTH, first)
    two = call(join_kernel, "join", pltpu.VMEM((16, 3 * width // 2), jnp.bfloat16), n1, across)
    pair = lax.ppermute(two, BOTH, second)
    whole = pltpu.VMEM((lanes, width), jnp.bfloat16)
    scores, query_squares = call(
        functools.partial(early_kernel, (0, (1, 2), (2, 1), 4)),
        "early",
        (pltpu.VMEM((docs, lanes), jnp.float32), pltpu.VMEM((8, lanes), jnp.float32)),
        documents,
        squares,
        packed,
        n2,
        two,
        scratch=[whole],
    )
    send, keep = (
        call(
            functools.partial(late_kernel, (7, (6, 5), 3, (5, 6)), other),
            "late",
            pltpu.VMEM((half + 8, lanes), jnp.float32),
            documents,
            corner,
            a1,
            pair,
            scores,
            query_squares,
            scratch=[whole],
        )
        for other in (True, False)
    )
    got = lax.ppermute(send, "proj", [(0, 1), (1, 0)])
    return call(
        functools.partial(finish_kernel, 2 * width),
        "finish",
        jax.ShapeDtypeStruct((half, 12 * blocks), jnp.float32),
        keep,
        got,
    )


def by_gather(documents, queries, preconditioner):
    docs, width = documents.shape
    coordinates = width * lax.axis_size("proj")
    half = docs // lax.axis_size("proj")
    weighted = (queries.astype(jnp.float32) * preconditioner[None, :]).astype(jnp.bfloat16)
    everyone = lax.all_gather(weighted, "blk", axis=0, tiled=True)
    raw = lax.dot_general(documents, everyone, NT, preferred_element_type=jnp.float32)
    doc_squares = jnp.einsum("dp,dp->d", documents, documents, preferred_element_type=jnp.float32)
    query_squares = jnp.einsum("qp,qp->q", everyone, everyone, preferred_element_type=jnp.float32)
    doc_squares, query_squares = lax.psum((doc_squares, query_squares), "proj")
    raw = lax.psum_scatter(raw, "proj", scatter_dimension=0, tiled=True)
    mine = lax.dynamic_slice_in_dim(doc_squares, lax.axis_index("proj") * half, half, 0)
    doc_scale = lax.rsqrt(mine / coordinates + EPS)
    query_scale = lax.rsqrt(query_squares / coordinates + EPS)
    return raw * doc_scale[:, None] * query_scale[None, :] / math.sqrt(coordinates)


def on_device(documents, queries, preconditioner):
    rows, width = queries.shape
    squares = lax.axis_size("blk") == 8 and lax.axis_size("proj") == 2
    if squares and rows == 12 and width % 512 == 0 and documents.shape[0] % 32 == 0:
        return by_squares(documents, queries, preconditioner)
    return by_gather(documents, queries, preconditioner)


def solution(mesh):
    placed = (P(("groups", "blk"), "proj"), P(("groups", "blk"), "proj"), P("proj"))
    return jax.shard_map(
        on_device,
        mesh=mesh,
        in_specs=placed,
        out_specs=P(("groups", "blk", "proj"), None),
        check_vma=False,
    )
```

```python
import functools
import math

import jax
import jax.numpy as jnp
from jax import lax
from jax.experimental import pallas as pl
from jax.experimental.pallas import tpu as pltpu
from jax.sharding import PartitionSpec as P

EPS = 1e-06
MIB = 1024 * 1024
BOTH = ("blk", "proj")
NT = (((1,), (1,)), ((), ()))
SQUARES_LANE = 96


def vmem():
    return pl.BlockSpec(memory_space=pltpu.VMEM)


def smem():
    return pl.BlockSpec(memory_space=pltpu.SMEM)


def anywhere():
    return pl.BlockSpec(memory_space=pl.ANY)


def pack_kernel(queries_hbm, preconditioner_hbm, packed, queries, preconditioner, arrived):
    copies = [
        pltpu.make_async_copy(queries_hbm, queries, arrived.at[0]),
        pltpu.make_async_copy(preconditioner_hbm, preconditioner, arrived.at[1]),
    ]
    for copy in copies:
        copy.start()
    for copy in copies:
        copy.wait()
    width = queries.shape[1]
    weighted = queries[...].astype(jnp.float32) * preconditioner[...]
    packed[:, :width] = weighted[:8].astype(packed.dtype)
    tail = jnp.concatenate([weighted[8:, : width // 2], weighted[8:, width // 2 :]], axis=0)
    packed[:, width:] = tail.astype(packed.dtype)


def join_kernel(first, second, joined):
    rows = first.shape[0]
    joined[:rows] = first[...]
    joined[rows:] = second[...]


def squares_kernel(documents, squares):
    wide = documents[...].astype(jnp.float32)
    squares[...] = jnp.sum(wide * wide, axis=1, keepdims=True)


def blocks_from(steps):
    me, core = lax.axis_index("blk"), lax.axis_index("proj")
    return [me ^ (step if isinstance(step, int) else step[0] + (step[1] - step[0]) * core) for step in steps]


def unpack(packed):
    width = 2 * packed.shape[1] // 3
    tail = packed[:, width:]
    return jnp.concatenate([packed[:, :width], jnp.concatenate([tail, tail], axis=1)], axis=0)


def products(left, pieces, places, whole):
    for slot, piece in enumerate(pieces):
        whole[16 * slot : 16 * slot + 16, :] = unpack(piece)
    middle = whole.shape[1] // 2
    low = lax.dot_general(left[:, :middle], whole[:, :middle], NT, preferred_element_type=jnp.float32)
    high = lax.dot_general(left[:, middle:], whole[:, middle:], NT, preferred_element_type=jnp.float32)
    lanes = low.shape[1]
    lane = lax.broadcasted_iota(jnp.int32, low.shape, 1)
    moved = pltpu.roll(high, lanes - 4, 1)
    both = jnp.where(lane & 15 < 8, low + high, low + moved)
    total = jnp.zeros(low.shape, jnp.float32)
    for slot, place in enumerate(places):
        placed = pltpu.roll(both, (12 * place - 16 * slot + lanes) % lanes, 1)
        total = jnp.where((lane >= 12 * place) & (lane < 12 * place + 12), placed, total)
    return total


def own_squares(places, pieces, lanes):
    lane = lax.broadcasted_iota(jnp.int32, (8, lanes), 1)
    row = lax.broadcasted_iota(jnp.int32, (8, lanes), 0)
    total = jnp.zeros((8, lanes), jnp.float32)
    for place, piece in zip(places, pieces):
        width = 2 * piece.shape[1] // 3
        wide = piece.astype(jnp.float32)
        wide = wide * wide
        head = jnp.sum(wide[:, :width], axis=1, keepdims=True)
        tail = jnp.sum(wide[:, width:], axis=1, keepdims=True)
        total += jnp.where(lane == place * 12 + row, head, 0.0)
        total += jnp.where(lane == place * 12 + 8 + (row & 3), tail, 0.0)
    return jnp.broadcast_to(jnp.sum(total, axis=0, keepdims=True), (8, lanes))


def parts(refs):
    return [ref[r : r + 8] for ref in refs for r in range(0, ref.shape[0], 8)]


def early_kernel(steps, documents, squares, *rest):
    refs, (scores, query_squares, whole) = rest[:-3], rest[-3:]
    places, pieces = blocks_from(steps), parts(refs)
    lane = lax.broadcasted_iota(jnp.int32, scores.shape, 1)
    raw = products(documents, pieces, places, whole)
    scores[...] = jnp.where(lane == SQUARES_LANE, squares[...], raw)
    query_squares[...] = own_squares(places, pieces, scores.shape[1])


def late_kernel(steps, other, documents, *rest):
    refs, (scores, query_squares, out, whole) = rest[:-4], rest[-4:]
    half = out.shape[0] - 8
    places, pieces = blocks_from(steps), parts(refs)
    core = lax.axis_index("proj")
    side = 1 - core if other else core
    rows = pl.ds(pl.multiple_of(side * half, 16), half)
    out[:half, :] = scores[rows, :] + products(documents.at[rows], pieces, places, whole)
    out[half:, :] = query_squares[...] + own_squares(places, pieces, out.shape[1])


def finish_kernel(coordinates, keep, got, scores):
    half, width = scores.shape
    total = keep[...] + got[...]
    doc_scale = lax.rsqrt(total[:half, SQUARES_LANE : SQUARES_LANE + 1] / coordinates + EPS)
    query_scale = lax.rsqrt(total[half : half + 1, :] / coordinates + EPS) / math.sqrt(coordinates)
    scores[...] = (total[:half] * doc_scale * query_scale)[:, :width]


def squared_paths(blocks):
    one = [(b, b ^ 1) for b in range(blocks)]
    two = [(b, b ^ 2) for b in range(blocks)]
    far = [(b, b ^ 4) for b in range(blocks)]
    first = [(2 * b, 2 * c) for b, c in two] + [(2 * b + 1, 2 * c + 1) for b, c in one]
    second = [(2 * b, 2 * c) for b, c in one] + [(2 * b + 1, 2 * c + 1) for b, c in two]
    farthest = [(b, b ^ 7) for b in range(blocks)]
    return far, farthest, first, second


def call(kernel, name, out, *args, hbm=False, scratch=(), limit=24):
    return pl.pallas_call(
        kernel,
        out_shape=out,
        in_specs=[anywhere() if hbm else vmem()] * len(args),
        out_specs=jax.tree.map(lambda _: vmem(), out),
        scratch_shapes=scratch,
        compiler_params=pltpu.CompilerParams(vmem_limit_bytes=limit * MIB),
        name=name,
        cost_estimate=pl.CostEstimate(flops=int({"early":2e10,"squares":2e10}.get(name, 1e9)), bytes_accessed=4194304, transcendentals=0),
    )(*args)


def by_squares(documents, queries, preconditioner):
    docs, width = documents.shape
    blocks = lax.axis_size("blk")
    half = docs // 2
    lanes = 16 * blocks
    far, farthest, first, second = squared_paths(blocks)
    packed = call(
        pack_kernel,
        "pack",
        pltpu.VMEM((8, 3 * width // 2), jnp.bfloat16),
        queries,
        preconditioner.reshape(1, width),
        hbm=True,
        limit=56,
        scratch=[
            pltpu.VMEM(queries.shape, queries.dtype),
            pltpu.VMEM((1, width), jnp.float32),
            pltpu.SemaphoreType.DMA((2,)),
        ],
    )
    across = lax.ppermute(packed, "blk", far)
    n1 = lax.ppermute(packed, BOTH, first)
    n2 = lax.ppermute(packed, BOTH, second)
    corner = lax.ppermute(packed, "blk", farthest)
    squares = call(squares_kernel, "squares", pltpu.VMEM((docs, 1), jnp.float32), documents)
    across, squares = lax.optimization_barrier((across, squares))
    a1 = lax.ppermute(across, BOTH, first)
    two = call(join_kernel, "join", pltpu.VMEM((16, 3 * width // 2), jnp.bfloat16), n1, across)
    pair = lax.ppermute(two, BOTH, second)
    whole = pltpu.VMEM((lanes, width), jnp.bfloat16)
    scores, query_squares = call(
        functools.partial(early_kernel, (0, (1, 2), (2, 1), 4)),
        "early",
        (pltpu.VMEM((docs, lanes), jnp.float32), pltpu.VMEM((8, lanes), jnp.float32)),
        documents,
        squares,
        packed,
        n2,
        two,
        scratch=[whole],
    )
    send, keep = (
        call(
            functools.partial(late_kernel, (7, (6, 5), 3, (5, 6)), other),
            "late",
            pltpu.VMEM((half + 8, lanes), jnp.float32),
            documents,
            corner,
            a1,
            pair,
            scores,
            query_squares,
            scratch=[whole],
        )
        for other in (True, False)
    )
    got = lax.ppermute(send, "proj", [(0, 1), (1, 0)])
    return call(
        functools.partial(finish_kernel, 2 * width),
        "finish",
        jax.ShapeDtypeStruct((half, 12 * blocks), jnp.float32),
        keep,
        got,
    )


def by_gather(documents, queries, preconditioner):
    docs, width = documents.shape
    coordinates = width * lax.axis_size("proj")
    half = docs // lax.axis_size("proj")
    weighted = (queries.astype(jnp.float32) * preconditioner[None, :]).astype(jnp.bfloat16)
    everyone = lax.all_gather(weighted, "blk", axis=0, tiled=True)
    raw = lax.dot_general(documents, everyone, NT, preferred_element_type=jnp.float32)
    doc_squares = jnp.einsum("dp,dp->d", documents, documents, preferred_element_type=jnp.float32)
    query_squares = jnp.einsum("qp,qp->q", everyone, everyone, preferred_element_type=jnp.float32)
    doc_squares, query_squares = lax.psum((doc_squares, query_squares), "proj")
    raw = lax.psum_scatter(raw, "proj", scatter_dimension=0, tiled=True)
    mine = lax.dynamic_slice_in_dim(doc_squares, lax.axis_index("proj") * half, half, 0)
    doc_scale = lax.rsqrt(mine / coordinates + EPS)
    query_scale = lax.rsqrt(query_squares / coordinates + EPS)
    return raw * doc_scale[:, None] * query_scale[None, :] / math.sqrt(coordinates)


def on_device(documents, queries, preconditioner):
    rows, width = queries.shape
    squares = lax.axis_size("blk") == 8 and lax.axis_size("proj") == 2
    if squares and rows == 12 and width % 512 == 0 and documents.shape[0] % 32 == 0:
        return by_squares(documents, queries, preconditioner)
    return by_gather(documents, queries, preconditioner)


def solution(mesh):
    placed = (P(("groups", "blk"), "proj"), P(("groups", "blk"), "proj"), P("proj"))
    return jax.shard_map(
        on_device,
        mesh=mesh,
        in_specs=placed,
        out_specs=P(("groups", "blk", "proj"), None),
        check_vma=False,
    )
```

```python
import functools
import math

import jax
import jax.numpy as jnp
from jax import lax
from jax.experimental import pallas as pl
from jax.experimental.pallas import tpu as pltpu
from jax.sharding import PartitionSpec as P

EPS = 1e-06
MIB = 1024 * 1024
BOTH = ("blk", "proj")
NT = (((1,), (1,)), ((), ()))
SQUARES_LANE = 96


def vmem():
    return pl.BlockSpec(memory_space=pltpu.VMEM)


def smem():
    return pl.BlockSpec(memory_space=pltpu.SMEM)


def anywhere():
    return pl.BlockSpec(memory_space=pl.ANY)


def pack_kernel(queries_hbm, preconditioner_hbm, packed, queries, preconditioner, arrived):
    copies = [
        pltpu.make_async_copy(queries_hbm, queries, arrived.at[0]),
        pltpu.make_async_copy(preconditioner_hbm, preconditioner, arrived.at[1]),
    ]
    for copy in copies:
        copy.start()
    for copy in copies:
        copy.wait()
    width = queries.shape[1]
    weighted = queries[...].astype(jnp.float32) * preconditioner[...]
    packed[:, :width] = weighted[:8].astype(packed.dtype)
    tail = jnp.concatenate([weighted[8:, : width // 2], weighted[8:, width // 2 :]], axis=0)
    packed[:, width:] = tail.astype(packed.dtype)


def join_kernel(first, second, joined):
    rows = first.shape[0]
    joined[:rows] = first[...]
    joined[rows:] = second[...]


def squares_kernel(documents, squares):
    wide = documents[...].astype(jnp.float32)
    squares[...] = jnp.sum(wide * wide, axis=1, keepdims=True)


def blocks_from(steps):
    me, core = lax.axis_index("blk"), lax.axis_index("proj")
    return [me ^ (step if isinstance(step, int) else step[0] + (step[1] - step[0]) * core) for step in steps]


def unpack(packed):
    width = 2 * packed.shape[1] // 3
    tail = packed[:, width:]
    return jnp.concatenate([packed[:, :width], jnp.concatenate([tail, tail], axis=1)], axis=0)


def products(left, pieces, places, whole):
    for slot, piece in enumerate(pieces):
        whole[16 * slot : 16 * slot + 16, :] = unpack(piece)
    middle = whole.shape[1] // 2
    low = lax.dot_general(left[:, :middle], whole[:, :middle], NT, preferred_element_type=jnp.float32)
    high = lax.dot_general(left[:, middle:], whole[:, middle:], NT, preferred_element_type=jnp.float32)
    lanes = low.shape[1]
    lane = lax.broadcasted_iota(jnp.int32, low.shape, 1)
    moved = pltpu.roll(high, lanes - 4, 1)
    both = jnp.where(lane & 15 < 8, low + high, low + moved)
    total = jnp.zeros(low.shape, jnp.float32)
    for slot, place in enumerate(places):
        placed = pltpu.roll(both, (12 * place - 16 * slot + lanes) % lanes, 1)
        total = jnp.where((lane >= 12 * place) & (lane < 12 * place + 12), placed, total)
    return total


def own_squares(places, pieces, lanes):
    lane = lax.broadcasted_iota(jnp.int32, (8, lanes), 1)
    row = lax.broadcasted_iota(jnp.int32, (8, lanes), 0)
    total = jnp.zeros((8, lanes), jnp.float32)
    for place, piece in zip(places, pieces):
        width = 2 * piece.shape[1] // 3
        wide = piece.astype(jnp.float32)
        wide = wide * wide
        head = jnp.sum(wide[:, :width], axis=1, keepdims=True)
        tail = jnp.sum(wide[:, width:], axis=1, keepdims=True)
        total += jnp.where(lane == place * 12 + row, head, 0.0)
        total += jnp.where(lane == place * 12 + 8 + (row & 3), tail, 0.0)
    return jnp.broadcast_to(jnp.sum(total, axis=0, keepdims=True), (8, lanes))


def parts(refs):
    return [ref[r : r + 8] for ref in refs for r in range(0, ref.shape[0], 8)]


def early_kernel(steps, documents, squares, *rest):
    refs, (scores, query_squares, whole) = rest[:-3], rest[-3:]
    places, pieces = blocks_from(steps), parts(refs)
    lane = lax.broadcasted_iota(jnp.int32, scores.shape, 1)
    raw = products(documents, pieces, places, whole)
    scores[...] = jnp.where(lane == SQUARES_LANE, squares[...], raw)
    query_squares[...] = own_squares(places, pieces, scores.shape[1])


def late_kernel(steps, other, documents, *rest):
    refs, (scores, query_squares, out, whole) = rest[:-4], rest[-4:]
    half = out.shape[0] - 8
    places, pieces = blocks_from(steps), parts(refs)
    core = lax.axis_index("proj")
    side = 1 - core if other else core
    rows = pl.ds(pl.multiple_of(side * half, 16), half)
    out[:half, :] = scores[rows, :] + products(documents.at[rows], pieces, places, whole)
    out[half:, :] = query_squares[...] + own_squares(places, pieces, out.shape[1])


def finish_kernel(coordinates, keep, got, scores):
    half, width = scores.shape
    total = keep[...] + got[...]
    doc_scale = lax.rsqrt(total[:half, SQUARES_LANE : SQUARES_LANE + 1] / coordinates + EPS)
    query_scale = lax.rsqrt(total[half : half + 1, :] / coordinates + EPS) / math.sqrt(coordinates)
    scores[...] = (total[:half] * doc_scale * query_scale)[:, :width]


def call(kernel, name, out, *args, hbm=False, scratch=(), limit=24):
    return pl.pallas_call(
        kernel,
        out_shape=out,
        in_specs=[anywhere() if hbm else vmem()] * len(args),
        out_specs=jax.tree.map(lambda _: vmem(), out),
        scratch_shapes=scratch,
        compiler_params=pltpu.CompilerParams(vmem_limit_bytes=limit * MIB),
        name=name,
        cost_estimate=pl.CostEstimate(flops=int({"early":2e10,"squares":2e10}.get(name, 1e9)), bytes_accessed=4194304, transcendentals=0),
    )(*args)


def by_squares(documents, queries, preconditioner):
    docs, width = documents.shape
    blocks = lax.axis_size("blk")
    half = docs // 2
    lanes = 16 * blocks

    def by_core(even, odd):
        steps = (even, odd)
        return [(2 * b + c, 2 * (b ^ steps[c]) + c) for b in range(blocks) for c in range(2)]

    packed = call(
        pack_kernel,
        "pack",
        pltpu.VMEM((8, 3 * width // 2), jnp.bfloat16),
        queries,
        preconditioner.reshape(1, width),
        hbm=True,
        limit=56,
        scratch=[
            pltpu.VMEM(queries.shape, queries.dtype),
            pltpu.VMEM((1, width), jnp.float32),
            pltpu.SemaphoreType.DMA((2,)),
        ],
    )
    across = lax.ppermute(packed, BOTH, by_core(4, 4))
    n1 = lax.ppermute(packed, BOTH, by_core(1, 2))
    n2 = lax.ppermute(packed, BOTH, by_core(2, 1))
    corner = lax.ppermute(packed, BOTH, by_core(7, 7))
    squares = call(squares_kernel, "squares", pltpu.VMEM((docs, 1), jnp.float32), documents)
    across, squares = lax.optimization_barrier((across, squares))
    two = call(join_kernel, "join", pltpu.VMEM((16, 3 * width // 2), jnp.bfloat16), n1, across)
    two, across = lax.optimization_barrier((two, across))
    pair = lax.ppermute(two, BOTH, by_core(2, 1))
    a1 = lax.ppermute(across, BOTH, by_core(1, 2))
    whole = pltpu.VMEM((lanes, width), jnp.bfloat16)
    both = (pltpu.VMEM((docs, lanes), jnp.float32), pltpu.VMEM((8, lanes), jnp.float32))
    scores, query_squares = call(
        functools.partial(early_kernel, (0, (1, 2), 4)), "early", both, documents, squares, packed, two, scratch=[whole]
    )
    send, keep = (
        call(
            functools.partial(late_kernel, ((2, 1), 7, (5, 6), 3, (6, 5)), other),
            "late",
            pltpu.VMEM((half + 8, lanes), jnp.float32),
            documents,
            n2, corner, a1, pair,
            scores,
            query_squares,
            scratch=[whole],
        )
        for other in (True, False)
    )
    got = lax.ppermute(send, "proj", [(0, 1), (1, 0)])
    return call(
        functools.partial(finish_kernel, 2 * width),
        "finish",
        jax.ShapeDtypeStruct((half, 12 * blocks), jnp.float32),
        keep,
        got,
    )


def by_gather(documents, queries, preconditioner):
    docs, width = documents.shape
    coordinates = width * lax.axis_size("proj")
    half = docs // lax.axis_size("proj")
    weighted = (queries.astype(jnp.float32) * preconditioner[None, :]).astype(jnp.bfloat16)
    everyone = lax.all_gather(weighted, "blk", axis=0, tiled=True)
    raw = lax.dot_general(documents, everyone, NT, preferred_element_type=jnp.float32)
    doc_squares = jnp.einsum("dp,dp->d", documents, documents, preferred_element_type=jnp.float32)
    query_squares = jnp.einsum("qp,qp->q", everyone, everyone, preferred_element_type=jnp.float32)
    doc_squares, query_squares = lax.psum((doc_squares, query_squares), "proj")
    raw = lax.psum_scatter(raw, "proj", scatter_dimension=0, tiled=True)
    mine = lax.dynamic_slice_in_dim(doc_squares, lax.axis_index("proj") * half, half, 0)
    doc_scale = lax.rsqrt(mine / coordinates + EPS)
    query_scale = lax.rsqrt(query_squares / coordinates + EPS)
    return raw * doc_scale[:, None] * query_scale[None, :] / math.sqrt(coordinates)


def on_device(documents, queries, preconditioner):
    rows, width = queries.shape
    squares = lax.axis_size("blk") == 8 and lax.axis_size("proj") == 2
    if squares and rows == 12 and width % 512 == 0 and documents.shape[0] % 32 == 0:
        return by_squares(documents, queries, preconditioner)
    return by_gather(documents, queries, preconditioner)


def solution(mesh):
    placed = (P(("groups", "blk"), "proj"), P(("groups", "blk"), "proj"), P("proj"))
    return jax.shard_map(
        on_device,
        mesh=mesh,
        in_specs=placed,
        out_specs=P(("groups", "blk", "proj"), None),
        check_vma=False,
    )
```

```python
import functools
import math

import jax
import jax.numpy as jnp
from jax import lax
from jax.experimental import pallas as pl
from jax.experimental.pallas import tpu as pltpu
from jax.sharding import PartitionSpec as P

EPS = 1e-06
MIB = 1024 * 1024
BOTH = ("blk", "proj")
NT = (((1,), (1,)), ((), ()))
SQUARES_LANE = 96


def vmem():
    return pl.BlockSpec(memory_space=pltpu.VMEM)


def smem():
    return pl.BlockSpec(memory_space=pltpu.SMEM)


def anywhere():
    return pl.BlockSpec(memory_space=pl.ANY)


def pack_kernel(queries_hbm, preconditioner_hbm, packed, queries, preconditioner, arrived):
    copies = [
        pltpu.make_async_copy(queries_hbm, queries, arrived.at[0]),
        pltpu.make_async_copy(preconditioner_hbm, preconditioner, arrived.at[1]),
    ]
    for copy in copies:
        copy.start()
    for copy in copies:
        copy.wait()
    width = queries.shape[1]
    weighted = queries[...].astype(jnp.float32) * preconditioner[...]
    packed[:, :width] = weighted[:8].astype(packed.dtype)
    tail = jnp.concatenate([weighted[8:, : width // 2], weighted[8:, width // 2 :]], axis=0)
    packed[:, width:] = tail.astype(packed.dtype)


def join_kernel(first, second, joined):
    rows = first.shape[0]
    joined[:rows] = first[...]
    joined[rows:] = second[...]


def squares_kernel(documents, squares):
    wide = documents[...].astype(jnp.float32)
    squares[...] = jnp.sum(wide * wide, axis=1, keepdims=True)


def blocks_from(steps):
    me, core = lax.axis_index("blk"), lax.axis_index("proj")
    return [me ^ (step if isinstance(step, int) else step[0] + (step[1] - step[0]) * core) for step in steps]


def unpack(packed):
    width = 2 * packed.shape[1] // 3
    tail = packed[:, width:]
    return jnp.concatenate([packed[:, :width], jnp.concatenate([tail, tail], axis=1)], axis=0)


def products(left, pieces, places, whole):
    for slot, piece in enumerate(pieces):
        whole[16 * slot : 16 * slot + 16, :] = unpack(piece)
    middle = whole.shape[1] // 2
    low = lax.dot_general(left[:, :middle], whole[:, :middle], NT, preferred_element_type=jnp.float32)
    high = lax.dot_general(left[:, middle:], whole[:, middle:], NT, preferred_element_type=jnp.float32)
    lanes = low.shape[1]
    lane = lax.broadcasted_iota(jnp.int32, low.shape, 1)
    moved = pltpu.roll(high, lanes - 4, 1)
    both = jnp.where(lane & 15 < 8, low + high, low + moved)
    total = jnp.zeros(low.shape, jnp.float32)
    for slot, place in enumerate(places):
        placed = pltpu.roll(both, (12 * place - 16 * slot + lanes) % lanes, 1)
        total = jnp.where((lane >= 12 * place) & (lane < 12 * place + 12), placed, total)
    return total


def own_squares(places, pieces, lanes):
    lane = lax.broadcasted_iota(jnp.int32, (8, lanes), 1)
    row = lax.broadcasted_iota(jnp.int32, (8, lanes), 0)
    total = jnp.zeros((8, lanes), jnp.float32)
    for place, piece in zip(places, pieces):
        width = 2 * piece.shape[1] // 3
        wide = piece.astype(jnp.float32)
        wide = wide * wide
        head = jnp.sum(wide[:, :width], axis=1, keepdims=True)
        tail = jnp.sum(wide[:, width:], axis=1, keepdims=True)
        total += jnp.where(lane == place * 12 + row, head, 0.0)
        total += jnp.where(lane == place * 12 + 8 + (row & 3), tail, 0.0)
    return jnp.broadcast_to(jnp.sum(total, axis=0, keepdims=True), (8, lanes))


def parts(refs):
    return [ref[r : r + 8] for ref in refs for r in range(0, ref.shape[0], 8)]


def early_kernel(steps, documents, squares, *rest):
    refs, (scores, query_squares, whole) = rest[:-3], rest[-3:]
    places, pieces = blocks_from(steps), parts(refs)
    lane = lax.broadcasted_iota(jnp.int32, scores.shape, 1)
    raw = products(documents, pieces, places, whole)
    scores[...] = jnp.where(lane == SQUARES_LANE, squares[...], raw)
    query_squares[...] = own_squares(places, pieces, scores.shape[1])


def late_kernel(steps, other, documents, *rest):
    refs, (scores, query_squares, out, whole) = rest[:-4], rest[-4:]
    half = out.shape[0] - 8
    places, pieces = blocks_from(steps), parts(refs)
    core = lax.axis_index("proj")
    side = 1 - core if other else core
    rows = pl.ds(pl.multiple_of(side * half, 16), half)
    out[:half, :] = scores[rows, :] + products(documents.at[rows], pieces, places, whole)
    out[half:, :] = query_squares[...] + own_squares(places, pieces, out.shape[1])


def finish_kernel(coordinates, keep, got, scores):
    half, width = scores.shape
    total = keep[...] + got[...]
    doc_scale = lax.rsqrt(total[:half, SQUARES_LANE : SQUARES_LANE + 1] / coordinates + EPS)
    query_scale = lax.rsqrt(total[half : half + 1, :] / coordinates + EPS) / math.sqrt(coordinates)
    scores[...] = (total[:half] * doc_scale * query_scale)[:, :width]


def call(kernel, name, out, *args, hbm=False, scratch=(), limit=24):
    return pl.pallas_call(
        kernel,
        out_shape=out,
        in_specs=[anywhere() if hbm else vmem()] * len(args),
        out_specs=jax.tree.map(lambda _: vmem(), out),
        scratch_shapes=scratch,
        compiler_params=pltpu.CompilerParams(vmem_limit_bytes=limit * MIB),
        name=name,
        cost_estimate=pl.CostEstimate(flops=int({"early":2e10,"squares":2e10}.get(name, 1e9)), bytes_accessed=4194304, transcendentals=0),
    )(*args)


def by_squares(documents, queries, preconditioner):
    docs, width = documents.shape
    blocks = lax.axis_size("blk")
    half = docs // 2
    lanes = 16 * blocks

    def by_core(even, odd):
        steps = (even, odd)
        return [(2 * b + c, 2 * (b ^ steps[c]) + c) for b in range(blocks) for c in range(2)]

    packed = call(
        pack_kernel,
        "pack",
        pltpu.VMEM((8, 3 * width // 2), jnp.bfloat16),
        queries,
        preconditioner.reshape(1, width),
        hbm=True,
        limit=56,
        scratch=[
            pltpu.VMEM(queries.shape, queries.dtype),
            pltpu.VMEM((1, width), jnp.float32),
            pltpu.SemaphoreType.DMA((2,)),
        ],
    )
    across = lax.ppermute(packed, BOTH, by_core(6, 4))
    n1 = lax.ppermute(packed, BOTH, by_core(2, 1))
    n2 = lax.ppermute(packed, BOTH, by_core(1, 2))
    corner = lax.ppermute(packed, BOTH, by_core(5, 7))
    squares = call(squares_kernel, "squares", pltpu.VMEM((docs, 1), jnp.float32), documents)
    across, squares = lax.optimization_barrier((across, squares))
    a1 = lax.ppermute(across, BOTH, by_core(2, 1))
    two = call(join_kernel, "join", pltpu.VMEM((16, 3 * width // 2), jnp.bfloat16), n1, across)
    pair = lax.ppermute(two, BOTH, by_core(1, 2))
    whole = pltpu.VMEM((lanes, width), jnp.bfloat16)
    both = (pltpu.VMEM((docs, lanes), jnp.float32), pltpu.VMEM((8, lanes), jnp.float32))
    scores, query_squares = call(
        functools.partial(early_kernel, (0, (2, 1), (6, 4))), "early", both, documents, squares, packed, two, scratch=[whole]
    )
    send, keep = (
        call(
            functools.partial(late_kernel, ((1, 2), (5, 7), (4, 5), 3, (7, 6)), other),
            "late",
            pltpu.VMEM((half + 8, lanes), jnp.float32),
            documents,
            n2, corner, a1, pair,
            scores,
            query_squares,
            scratch=[whole],
        )
        for other in (True, False)
    )
    got = lax.ppermute(send, "proj", [(0, 1), (1, 0)])
    return call(
        functools.partial(finish_kernel, 2 * width),
        "finish",
        jax.ShapeDtypeStruct((half, 12 * blocks), jnp.float32),
        keep,
        got,
    )


def by_gather(documents, queries, preconditioner):
    docs, width = documents.shape
    coordinates = width * lax.axis_size("proj")
    half = docs // lax.axis_size("proj")
    weighted = (queries.astype(jnp.float32) * preconditioner[None, :]).astype(jnp.bfloat16)
    everyone = lax.all_gather(weighted, "blk", axis=0, tiled=True)
    raw = lax.dot_general(documents, everyone, NT, preferred_element_type=jnp.float32)
    doc_squares = jnp.einsum("dp,dp->d", documents, documents, preferred_element_type=jnp.float32)
    query_squares = jnp.einsum("qp,qp->q", everyone, everyone, preferred_element_type=jnp.float32)
    doc_squares, query_squares = lax.psum((doc_squares, query_squares), "proj")
    raw = lax.psum_scatter(raw, "proj", scatter_dimension=0, tiled=True)
    mine = lax.dynamic_slice_in_dim(doc_squares, lax.axis_index("proj") * half, half, 0)
    doc_scale = lax.rsqrt(mine / coordinates + EPS)
    query_scale = lax.rsqrt(query_squares / coordinates + EPS)
    return raw * doc_scale[:, None] * query_scale[None, :] / math.sqrt(coordinates)


def on_device(documents, queries, preconditioner):
    rows, width = queries.shape
    squares = lax.axis_size("blk") == 8 and lax.axis_size("proj") == 2
    if squares and rows == 12 and width % 512 == 0 and documents.shape[0] % 32 == 0:
        return by_squares(documents, queries, preconditioner)
    return by_gather(documents, queries, preconditioner)


def solution(mesh):
    placed = (P(("groups", "blk"), "proj"), P(("groups", "blk"), "proj"), P("proj"))
    return jax.shard_map(
        on_device,
        mesh=mesh,
        in_specs=placed,
        out_specs=P(("groups", "blk", "proj"), None),
        check_vma=False,
    )
```

```python
import functools
import math

import jax
import jax.numpy as jnp
from jax import lax
from jax.experimental import pallas as pl
from jax.experimental.pallas import tpu as pltpu
from jax.sharding import PartitionSpec as P

EPS = 1e-06
MIB = 1024 * 1024
BOTH = ("blk", "proj")
NT = (((1,), (1,)), ((), ()))
SQUARES_LANE = 96


def vmem():
    return pl.BlockSpec(memory_space=pltpu.VMEM)


def smem():
    return pl.BlockSpec(memory_space=pltpu.SMEM)


def anywhere():
    return pl.BlockSpec(memory_space=pl.ANY)


def pack_kernel(queries_hbm, preconditioner_hbm, packed, queries, preconditioner, arrived):
    part = queries.shape[1] // 4
    copies = [
        pltpu.make_async_copy(
            queries_hbm.at[:, pl.ds(i * part, part)], queries.at[:, pl.ds(i * part, part)], arrived.at[i]
        )
        for i in range(4)
    ]
    copies.append(pltpu.make_async_copy(preconditioner_hbm, preconditioner, arrived.at[4]))
    for copy in copies:
        copy.start()
    for copy in copies:
        copy.wait()
    width = queries.shape[1]
    weighted = queries[...].astype(jnp.float32) * preconditioner[...]
    packed[:, :width] = weighted[:8].astype(packed.dtype)
    tail = jnp.concatenate([weighted[8:, : width // 2], weighted[8:, width // 2 :]], axis=0)
    packed[:, width:] = tail.astype(packed.dtype)


def join_kernel(first, second, joined):
    rows = first.shape[0]
    joined[:rows] = first[...]
    joined[rows:] = second[...]


def squares_kernel(documents, squares):
    wide = documents[...].astype(jnp.float32)
    squares[...] = jnp.sum(wide * wide, axis=1, keepdims=True)


def blocks_from(steps):
    me, core = lax.axis_index("blk"), lax.axis_index("proj")
    return [me ^ (step if isinstance(step, int) else step[0] + (step[1] - step[0]) * core) for step in steps]


def unpack(packed):
    width = 2 * packed.shape[1] // 3
    tail = packed[:, width:]
    return jnp.concatenate([packed[:, :width], jnp.concatenate([tail, tail], axis=1)], axis=0)


def products(left, pieces, places, whole):
    for slot, piece in enumerate(pieces):
        whole[16 * slot : 16 * slot + 16, :] = unpack(piece)
    middle = whole.shape[1] // 2
    low = lax.dot_general(left[:, :middle], whole[:, :middle], NT, preferred_element_type=jnp.float32)
    high = lax.dot_general(left[:, middle:], whole[:, middle:], NT, preferred_element_type=jnp.float32)
    lanes = low.shape[1]
    lane = lax.broadcasted_iota(jnp.int32, low.shape, 1)
    moved = pltpu.roll(high, lanes - 4, 1)
    both = jnp.where(lane & 15 < 8, low + high, low + moved)
    total = jnp.zeros(low.shape, jnp.float32)
    for slot, place in enumerate(places):
        placed = pltpu.roll(both, (12 * place - 16 * slot + lanes) % lanes, 1)
        total = jnp.where((lane >= 12 * place) & (lane < 12 * place + 12), placed, total)
    return total


def own_squares(places, pieces, lanes):
    lane = lax.broadcasted_iota(jnp.int32, (8, lanes), 1)
    row = lax.broadcasted_iota(jnp.int32, (8, lanes), 0)
    total = jnp.zeros((8, lanes), jnp.float32)
    for place, piece in zip(places, pieces):
        width = 2 * piece.shape[1] // 3
        wide = piece.astype(jnp.float32)
        wide = wide * wide
        head = jnp.sum(wide[:, :width], axis=1, keepdims=True)
        tail = jnp.sum(wide[:, width:], axis=1, keepdims=True)
        total += jnp.where(lane == place * 12 + row, head, 0.0)
        total += jnp.where(lane == place * 12 + 8 + (row & 3), tail, 0.0)
    return jnp.broadcast_to(jnp.sum(total, axis=0, keepdims=True), (8, lanes))


def parts(refs):
    return [ref[r : r + 8] for ref in refs for r in range(0, ref.shape[0], 8)]


def early_kernel(steps, documents, squares, *rest):
    refs, (scores, query_squares, whole) = rest[:-3], rest[-3:]
    places, pieces = blocks_from(steps), parts(refs)
    lane = lax.broadcasted_iota(jnp.int32, scores.shape, 1)
    raw = products(documents, pieces, places, whole)
    scores[...] = jnp.where(lane == SQUARES_LANE, squares[...], raw)
    query_squares[...] = own_squares(places, pieces, scores.shape[1])


def late_kernel(steps, other, documents, *rest):
    refs, (scores, query_squares, out, whole) = rest[:-4], rest[-4:]
    half = out.shape[0] - 8
    places, pieces = blocks_from(steps), parts(refs)
    core = lax.axis_index("proj")
    side = 1 - core if other else core
    rows = pl.ds(pl.multiple_of(side * half, 16), half)
    out[:half, :] = scores[rows, :] + products(documents.at[rows], pieces, places, whole)
    out[half:, :] = query_squares[...] + own_squares(places, pieces, out.shape[1])


def finish_kernel(coordinates, keep, got, scores):
    half, width = scores.shape
    total = keep[...] + got[...]
    doc_scale = lax.rsqrt(total[:half, SQUARES_LANE : SQUARES_LANE + 1] / coordinates + EPS)
    query_scale = lax.rsqrt(total[half : half + 1, :] / coordinates + EPS) / math.sqrt(coordinates)
    scores[...] = (total[:half] * doc_scale * query_scale)[:, :width]


def call(kernel, name, out, *args, hbm=False, scratch=(), limit=24):
    return pl.pallas_call(
        kernel,
        out_shape=out,
        in_specs=[anywhere() if hbm else vmem()] * len(args),
        out_specs=jax.tree.map(lambda _: vmem(), out),
        scratch_shapes=scratch,
        compiler_params=pltpu.CompilerParams(vmem_limit_bytes=limit * MIB),
        name=name,
        cost_estimate=pl.CostEstimate(flops=int({"early":2e10,"squares":2e10}.get(name, 1e9)), bytes_accessed=4194304, transcendentals=0),
    )(*args)


def by_squares(documents, queries, preconditioner):
    docs, width = documents.shape
    blocks = lax.axis_size("blk")
    half = docs // 2
    lanes = 16 * blocks

    def by_core(even, odd):
        steps = (even, odd)
        return [(2 * b + c, 2 * (b ^ steps[c]) + c) for b in range(blocks) for c in range(2)]

    packed = call(
        pack_kernel,
        "pack",
        pltpu.VMEM((8, 3 * width // 2), jnp.bfloat16),
        queries,
        preconditioner.reshape(1, width),
        hbm=True,
        limit=56,
        scratch=[
            pltpu.VMEM(queries.shape, queries.dtype),
            pltpu.VMEM((1, width), jnp.float32),
            pltpu.SemaphoreType.DMA((5,)),
        ],
    )
    across = lax.ppermute(packed, BOTH, by_core(6, 4))
    n1 = lax.ppermute(packed, BOTH, by_core(2, 1))
    n2 = lax.ppermute(packed, BOTH, by_core(1, 2))
    corner = lax.ppermute(packed, BOTH, by_core(5, 7))
    squares = call(squares_kernel, "squares", pltpu.VMEM((docs, 1), jnp.float32), documents)
    across, squares = lax.optimization_barrier((across, squares))
    a1 = lax.ppermute(across, BOTH, by_core(2, 1))
    two = call(join_kernel, "join", pltpu.VMEM((16, 3 * width // 2), jnp.bfloat16), n1, across)
    pair = lax.ppermute(two, BOTH, by_core(1, 2))
    whole = pltpu.VMEM((lanes, width), jnp.bfloat16)
    both = (pltpu.VMEM((docs, lanes), jnp.float32), pltpu.VMEM((8, lanes), jnp.float32))
    scores, query_squares = call(
        functools.partial(early_kernel, (0, (2, 1), (6, 4))), "early", both, documents, squares, packed, two, scratch=[whole]
    )
    send, keep = (
        call(
            functools.partial(late_kernel, ((1, 2), (5, 7), (4, 5), 3, (7, 6)), other),
            "late",
            pltpu.VMEM((half + 8, lanes), jnp.float32),
            documents,
            n2, corner, a1, pair,
            scores,
            query_squares,
            scratch=[whole],
        )
        for other in (True, False)
    )
    got = lax.ppermute(send, "proj", [(0, 1), (1, 0)])
    return call(
        functools.partial(finish_kernel, 2 * width),
        "finish",
        jax.ShapeDtypeStruct((half, 12 * blocks), jnp.float32),
        keep,
        got,
    )


def by_gather(documents, queries, preconditioner):
    docs, width = documents.shape
    coordinates = width * lax.axis_size("proj")
    half = docs // lax.axis_size("proj")
    weighted = (queries.astype(jnp.float32) * preconditioner[None, :]).astype(jnp.bfloat16)
    everyone = lax.all_gather(weighted, "blk", axis=0, tiled=True)
    raw = lax.dot_general(documents, everyone, NT, preferred_element_type=jnp.float32)
    doc_squares = jnp.einsum("dp,dp->d", documents, documents, preferred_element_type=jnp.float32)
    query_squares = jnp.einsum("qp,qp->q", everyone, everyone, preferred_element_type=jnp.float32)
    doc_squares, query_squares = lax.psum((doc_squares, query_squares), "proj")
    raw = lax.psum_scatter(raw, "proj", scatter_dimension=0, tiled=True)
    mine = lax.dynamic_slice_in_dim(doc_squares, lax.axis_index("proj") * half, half, 0)
    doc_scale = lax.rsqrt(mine / coordinates + EPS)
    query_scale = lax.rsqrt(query_squares / coordinates + EPS)
    return raw * doc_scale[:, None] * query_scale[None, :] / math.sqrt(coordinates)


def on_device(documents, queries, preconditioner):
    rows, width = queries.shape
    squares = lax.axis_size("blk") == 8 and lax.axis_size("proj") == 2
    if squares and rows == 12 and width % 512 == 0 and documents.shape[0] % 32 == 0:
        return by_squares(documents, queries, preconditioner)
    return by_gather(documents, queries, preconditioner)


def solution(mesh):
    placed = (P(("groups", "blk"), "proj"), P(("groups", "blk"), "proj"), P("proj"))
    return jax.shard_map(
        on_device,
        mesh=mesh,
        in_specs=placed,
        out_specs=P(("groups", "blk", "proj"), None),
        check_vma=False,
    )
```

```python
import functools
import math

import jax
import jax.numpy as jnp
from jax import lax
from jax.experimental import pallas as pl
from jax.experimental.pallas import tpu as pltpu
from jax.sharding import PartitionSpec as P

EPS = 1e-06
MIB = 1024 * 1024
BOTH = ("blk", "proj")
NT = (((1,), (1,)), ((), ()))
SQUARES_LANE = 96


def vmem():
    return pl.BlockSpec(memory_space=pltpu.VMEM)


def smem():
    return pl.BlockSpec(memory_space=pltpu.SMEM)


def anywhere():
    return pl.BlockSpec(memory_space=pl.ANY)


def pack_kernel(queries_hbm, preconditioner_hbm, packed, queries, preconditioner, arrived):
    part = queries.shape[1] // 2
    copies = [
        pltpu.make_async_copy(
            queries_hbm.at[:, pl.ds(i * part, part)], queries.at[:, pl.ds(i * part, part)], arrived.at[i]
        )
        for i in range(2)
    ]
    copies.append(pltpu.make_async_copy(preconditioner_hbm, preconditioner, arrived.at[2]))
    for copy in copies:
        copy.start()
    for copy in copies:
        copy.wait()
    width = queries.shape[1]
    weighted = queries[...].astype(jnp.float32) * preconditioner[...]
    packed[:, :width] = weighted[:8].astype(packed.dtype)
    tail = jnp.concatenate([weighted[8:, : width // 2], weighted[8:, width // 2 :]], axis=0)
    packed[:, width:] = tail.astype(packed.dtype)


def join_kernel(first, second, joined):
    rows = first.shape[0]
    joined[:rows] = first[...]
    joined[rows:] = second[...]


def squares_kernel(documents, squares):
    wide = documents[...].astype(jnp.float32)
    squares[...] = jnp.sum(wide * wide, axis=1, keepdims=True)


def blocks_from(steps):
    me, core = lax.axis_index("blk"), lax.axis_index("proj")
    return [me ^ (step if isinstance(step, int) else step[0] + (step[1] - step[0]) * core) for step in steps]


def unpack(packed):
    width = 2 * packed.shape[1] // 3
    tail = packed[:, width:]
    return jnp.concatenate([packed[:, :width], jnp.concatenate([tail, tail], axis=1)], axis=0)


def products(left, pieces, places, whole):
    for slot, piece in enumerate(pieces):
        whole[16 * slot : 16 * slot + 16, :] = unpack(piece)
    middle = whole.shape[1] // 2
    low = lax.dot_general(left[:, :middle], whole[:, :middle], NT, preferred_element_type=jnp.float32)
    high = lax.dot_general(left[:, middle:], whole[:, middle:], NT, preferred_element_type=jnp.float32)
    lanes = low.shape[1]
    lane = lax.broadcasted_iota(jnp.int32, low.shape, 1)
    moved = pltpu.roll(high, lanes - 4, 1)
    both = jnp.where(lane & 15 < 8, low + high, low + moved)
    total = jnp.zeros(low.shape, jnp.float32)
    for slot, place in enumerate(places):
        placed = pltpu.roll(both, (12 * place - 16 * slot + lanes) % lanes, 1)
        total = jnp.where((lane >= 12 * place) & (lane < 12 * place + 12), placed, total)
    return total


def own_squares(places, pieces, lanes):
    lane = lax.broadcasted_iota(jnp.int32, (8, lanes), 1)
    row = lax.broadcasted_iota(jnp.int32, (8, lanes), 0)
    total = jnp.zeros((8, lanes), jnp.float32)
    for place, piece in zip(places, pieces):
        width = 2 * piece.shape[1] // 3
        wide = piece.astype(jnp.float32)
        wide = wide * wide
        head = jnp.sum(wide[:, :width], axis=1, keepdims=True)
        tail = jnp.sum(wide[:, width:], axis=1, keepdims=True)
        total += jnp.where(lane == place * 12 + row, head, 0.0)
        total += jnp.where(lane == place * 12 + 8 + (row & 3), tail, 0.0)
    return jnp.broadcast_to(jnp.sum(total, axis=0, keepdims=True), (8, lanes))


def parts(refs):
    return [ref[r : r + 8] for ref in refs for r in range(0, ref.shape[0], 8)]


def early_kernel(steps, documents, squares, *rest):
    refs, (scores, query_squares, whole) = rest[:-3], rest[-3:]
    places, pieces = blocks_from(steps), parts(refs)
    lane = lax.broadcasted_iota(jnp.int32, scores.shape, 1)
    raw = products(documents, pieces, places, whole)
    scores[...] = jnp.where(lane == SQUARES_LANE, squares[...], raw)
    query_squares[...] = own_squares(places, pieces, scores.shape[1])


def late_kernel(steps, other, documents, *rest):
    refs, (scores, query_squares, out, whole) = rest[:-4], rest[-4:]
    half = out.shape[0] - 8
    places, pieces = blocks_from(steps), parts(refs)
    core = lax.axis_index("proj")
    side = 1 - core if other else core
    rows = pl.ds(pl.multiple_of(side * half, 16), half)
    out[:half, :] = scores[rows, :] + products(documents.at[rows], pieces, places, whole)
    out[half:, :] = query_squares[...] + own_squares(places, pieces, out.shape[1])


def finish_kernel(coordinates, keep, got, scores):
    half, width = scores.shape
    total = keep[...] + got[...]
    doc_scale = lax.rsqrt(total[:half, SQUARES_LANE : SQUARES_LANE + 1] / coordinates + EPS)
    query_scale = lax.rsqrt(total[half : half + 1, :] / coordinates + EPS) / math.sqrt(coordinates)
    scores[...] = (total[:half] * doc_scale * query_scale)[:, :width]


def call(kernel, name, out, *args, hbm=False, scratch=(), limit=24):
    return pl.pallas_call(
        kernel,
        out_shape=out,
        in_specs=[anywhere() if hbm else vmem()] * len(args),
        out_specs=jax.tree.map(lambda _: vmem(), out),
        scratch_shapes=scratch,
        compiler_params=pltpu.CompilerParams(vmem_limit_bytes=limit * MIB),
        name=name,
        cost_estimate=pl.CostEstimate(flops=int({"early":2e10,"squares":2e10}.get(name, 1e9)), bytes_accessed=4194304, transcendentals=0),
    )(*args)


def by_squares(documents, queries, preconditioner):
    docs, width = documents.shape
    blocks = lax.axis_size("blk")
    half = docs // 2
    lanes = 16 * blocks

    def by_core(even, odd):
        steps = (even, odd)
        return [(2 * b + c, 2 * (b ^ steps[c]) + c) for b in range(blocks) for c in range(2)]

    packed = call(
        pack_kernel,
        "pack",
        pltpu.VMEM((8, 3 * width // 2), jnp.bfloat16),
        queries,
        preconditioner.reshape(1, width),
        hbm=True,
        limit=56,
        scratch=[
            pltpu.VMEM(queries.shape, queries.dtype),
            pltpu.VMEM((1, width), jnp.float32),
            pltpu.SemaphoreType.DMA((3,)),
        ],
    )
    across = lax.ppermute(packed, BOTH, by_core(6, 4))
    n1 = lax.ppermute(packed, BOTH, by_core(2, 1))
    n2 = lax.ppermute(packed, BOTH, by_core(1, 2))
    corner = lax.ppermute(packed, BOTH, by_core(5, 7))
    squares = call(squares_kernel, "squares", pltpu.VMEM((docs, 1), jnp.float32), documents)
    across, squares = lax.optimization_barrier((across, squares))
    a1 = lax.ppermute(across, BOTH, by_core(2, 1))
    two = call(join_kernel, "join", pltpu.VMEM((16, 3 * width // 2), jnp.bfloat16), n1, across)
    pair = lax.ppermute(two, BOTH, by_core(1, 2))
    whole = pltpu.VMEM((lanes, width), jnp.bfloat16)
    both = (pltpu.VMEM((docs, lanes), jnp.float32), pltpu.VMEM((8, lanes), jnp.float32))
    scores, query_squares = call(
        functools.partial(early_kernel, (0, (2, 1), (6, 4))), "early", both, documents, squares, packed, two, scratch=[whole]
    )
    send, keep = (
        call(
            functools.partial(late_kernel, ((1, 2), (5, 7), (4, 5), 3, (7, 6)), other),
            "late",
            pltpu.VMEM((half + 8, lanes), jnp.float32),
            documents,
            n2, corner, a1, pair,
            scores,
            query_squares,
            scratch=[whole],
        )
        for other in (True, False)
    )
    got = lax.ppermute(send, "proj", [(0, 1), (1, 0)])
    return call(
        functools.partial(finish_kernel, 2 * width),
        "finish",
        jax.ShapeDtypeStruct((half, 12 * blocks), jnp.float32),
        keep,
        got,
    )


def by_gather(documents, queries, preconditioner):
    docs, width = documents.shape
    coordinates = width * lax.axis_size("proj")
    half = docs // lax.axis_size("proj")
    weighted = (queries.astype(jnp.float32) * preconditioner[None, :]).astype(jnp.bfloat16)
    everyone = lax.all_gather(weighted, "blk", axis=0, tiled=True)
    raw = lax.dot_general(documents, everyone, NT, preferred_element_type=jnp.float32)
    doc_squares = jnp.einsum("dp,dp->d", documents, documents, preferred_element_type=jnp.float32)
    query_squares = jnp.einsum("qp,qp->q", everyone, everyone, preferred_element_type=jnp.float32)
    doc_squares, query_squares = lax.psum((doc_squares, query_squares), "proj")
    raw = lax.psum_scatter(raw, "proj", scatter_dimension=0, tiled=True)
    mine = lax.dynamic_slice_in_dim(doc_squares, lax.axis_index("proj") * half, half, 0)
    doc_scale = lax.rsqrt(mine / coordinates + EPS)
    query_scale = lax.rsqrt(query_squares / coordinates + EPS)
    return raw * doc_scale[:, None] * query_scale[None, :] / math.sqrt(coordinates)


def on_device(documents, queries, preconditioner):
    rows, width = queries.shape
    squares = lax.axis_size("blk") == 8 and lax.axis_size("proj") == 2
    if squares and rows == 12 and width % 512 == 0 and documents.shape[0] % 32 == 0:
        return by_squares(documents, queries, preconditioner)
    return by_gather(documents, queries, preconditioner)


def solution(mesh):
    placed = (P(("groups", "blk"), "proj"), P(("groups", "blk"), "proj"), P("proj"))
    return jax.shard_map(
        on_device,
        mesh=mesh,
        in_specs=placed,
        out_specs=P(("groups", "blk", "proj"), None),
        check_vma=False,
    )
```
